32 devices in a mesh: row: 4 (over z), col: 8 (over y, x, core).
Axes of the slice: x: 2, y: 2, z: 4, core: 2. Of those that a mesh axis runs over, the one named last changes fastest.
Arguments:
- tile_values: float32 [4, 8, 128, 128, 128], P('row', 'col')
- tile_coords: int32 [4, 8, 128, 2], P('row', 'col'), may hold values from 0 to 143, as said below
- tile_count: int32 [4, 8], P('row', 'col'), may hold values from 16 to 128, as said below
- objective: float32 [65536], P('col')
- lower: float32 [65536], P('col'), may hold values from -2 to -0.2
- upper: float32 [65536], P('col'), may hold values from 0.2 to 2
- rhs: float32 [73728], P('row')
- primal_start: float32 [65536], P('col'), may hold values from -4 to 4
- dual_start: float32 [73728], P('row'), may hold values from 0 to 1
- step_size: float32 [1], replicated, may hold values from 0.02 to 0.06
Outputs:
- primal_solution: float32 [65536], P('col')
- dual_solution: float32 [73728], P('row')
The draws below stay inside these ranges and needn't reach their ends.
Inputs may be any that keep to these rules, and one draw needn't show every extreme that they name: `tile_coords`: coordinates are local: block rows 0 to 143, block columns 0 to 63, also in unused slots. Devices whose col index is congruent to their row index modulo the size of row hold one period: their block rows are (col index // size of row) * 64 plus 0 to 63. All other devices hold only linking block rows, 128 to 143. Every block row and every block column of A is met by some used slot. `tile_count`: period devices use all slots; other devices use 16 to 64 slots.
All inputs are finite; a program needn't handle non-finite values.
Results may differ from the reference program's by a relative error of at most 0.00012.
Values sent between devices are 32-bit elements; how exact they have to be, the bound alone decides.
A program may use at most 64 MiB of HBM per device.

```python
import math
import jax
import jax.numpy as jnp
from jax import lax

TILE = 128
CB_DEV = 64
LINK_DEV = 16
RUIZ = 2
ITERS = 2
TILES_DEV = 128
RB_DEV = 144
ROWS = 73728
COLS = 65536
N_ROW = 4
N_COL = 8


def distinct_order(key, grid, length):
    scores = jax.random.randint(key, grid + (length,), 0, 1 << 20) * length + jnp.arange(length, dtype=jnp.int32)
    return jnp.argsort(scores, axis=-1).astype(jnp.int32)


def tile_layout(key):
    base = jax.random.fold_in(key, 7)
    keys = jax.random.split(base, 8)
    grid = (N_ROW, N_COL)
    row_ids = jnp.arange(N_ROW, dtype=jnp.int32)[:, None]
    col_ids = jnp.arange(N_COL, dtype=jnp.int32)[None, :]
    diagonal = col_ids % N_ROW == row_ids
    period_start = (col_ids // N_ROW * CB_DEV)[:, :, None]
    cover_cols = distinct_order(keys[0], grid, CB_DEV)
    extra_rows = jax.random.randint(keys[1], grid + (TILES_DEV - CB_DEV,), 0, CB_DEV)
    extra_cols = jax.random.randint(keys[2], grid + (TILES_DEV - CB_DEV,), 0, CB_DEV)
    cover_rows = jnp.broadcast_to(jnp.arange(CB_DEV, dtype=jnp.int32), grid + (CB_DEV,))
    period_rows = jnp.concatenate([cover_rows, extra_rows], axis=-1) + period_start
    period_cols = jnp.concatenate([cover_cols, extra_cols], axis=-1)
    shuffle = distinct_order(keys[3], grid, TILES_DEV)
    period_rows = jnp.take_along_axis(period_rows, shuffle, axis=-1)
    period_cols = jnp.take_along_axis(period_cols, shuffle, axis=-1)
    link_start = CB_DEV * (N_COL // N_ROW)
    link_cover = distinct_order(keys[4], grid, LINK_DEV)
    link_extra = jax.random.randint(keys[5], grid + (TILES_DEV - LINK_DEV,), 0, LINK_DEV)
    link_rows = jnp.concatenate([link_cover, link_extra], axis=-1) + link_start
    link_cols = jax.random.randint(keys[6], grid + (TILES_DEV,), 0, CB_DEV)
    block_rows = jnp.where(diagonal[:, :, None], period_rows, link_rows).astype(jnp.int32)
    block_cols = jnp.where(diagonal[:, :, None], period_cols, link_cols).astype(jnp.int32)
    drawn = jax.random.randint(keys[7], grid, LINK_DEV, CB_DEV + 1)
    pinned = (row_ids == 0) & (col_ids == 1)
    drawn = jnp.where(pinned, LINK_DEV, drawn)
    counts = jnp.where(diagonal, TILES_DEV, drawn).astype(jnp.int32)
    return (block_rows, block_cols, counts)


def draw_tile_coords(key, part):
    block_rows, block_cols, counts = tile_layout(key)
    return jnp.stack([block_rows, block_cols], axis=-1)


def draw_tile_count(key, part):
    block_rows, block_cols, counts = tile_layout(key)
    return counts


def draw_tile_values(key, part):
    block_rows, block_cols, counts = tile_layout(key)
    global_rows = jnp.arange(N_ROW, dtype=jnp.int32)[:, None, None] * RB_DEV + block_rows
    global_cols = jnp.arange(N_COL, dtype=jnp.int32)[None, :, None] * CB_DEV + block_cols
    keys = jax.random.split(jax.random.fold_in(key, 19), 3)
    shape = (N_ROW, N_COL, TILES_DEV, TILE, TILE)
    row_table = jnp.exp(jax.random.uniform(keys[0], (N_ROW * RB_DEV, TILE), jnp.float32, math.log(0.3), math.log(3.0)))
    col_table = jnp.exp(jax.random.uniform(keys[1], (N_COL * CB_DEV, TILE), jnp.float32, math.log(0.3), math.log(3.0)))
    entries = jax.random.normal(keys[2], shape, jnp.float32)
    return entries * row_table[global_rows][..., :, None] * col_table[global_cols][..., None, :]


def rising_vector(key, length):
    keys = jax.random.split(key, 2)
    position = jnp.arange(length, dtype=jnp.float32) / length
    spread = jnp.exp(jax.random.uniform(keys[0], (length,), jnp.float32, 0.0, math.log(10.0)))
    values = jax.random.normal(keys[1], (length,), jnp.float32)
    return 0.3 * values * spread * jnp.exp(position * math.log(3.0))


def draw_objective(key, part):
    return rising_vector(jax.random.fold_in(key, 31), COLS)


def draw_rhs(key, part):
    return rising_vector(jax.random.fold_in(key, 43), ROWS)


def block_levels(rng, dims, cuts, smallest, top_value):
    loudness = 1.0
    for dim, shards_of in cuts:
        heights = jax.random.uniform(jax.random.fold_in(jax.random.fold_in(rng, 6), dim), (shards_of,), jnp.float32, smallest / len(cuts), top_value / len(cuts))
        loudness = loudness * jnp.repeat(jnp.exp(heights), dims[dim] // shards_of).reshape((-1,) + (1,) * (len(dims) - 1 - dim))
    return loudness


def scatter_about(own_key, shape, width, most, cuts=(), kind=jnp.bfloat16):
    level = block_levels(own_key, shape, cuts, -0.22, 0.18) if cuts else 1.0
    values = jax.random.normal(own_key, shape, jnp.float32) * width * level
    return jnp.minimum(jnp.maximum(values, -most), most).astype(kind)


def setup_inputs(seed: int = 0) -> dict:
    seeds = jax.random.split(jax.random.key(seed), 11)
    return {
        "tile_values": draw_tile_values(jax.random.fold_in(seeds[10], 71), 0),
        "tile_coords": draw_tile_coords(jax.random.fold_in(seeds[10], 71), 0),
        "tile_count": draw_tile_count(jax.random.fold_in(seeds[10], 71), 0),
        "objective": draw_objective(jax.random.fold_in(seeds[10], 71), 0),
        "lower": jnp.clip(-2.0 + 1.8 * jax.random.uniform(seeds[4], (COLS,), jnp.float32) ** block_levels(seeds[4], (COLS,), ((0, 8),), -0.2, 0.2), -2.0, -0.2),
        "upper": jnp.clip(0.2 + 1.8 * jax.random.uniform(seeds[5], (COLS,), jnp.float32) ** block_levels(seeds[5], (COLS,), ((0, 8),), -0.2, 0.2), 0.2, 2.0),
        "rhs": draw_rhs(jax.random.fold_in(seeds[10], 71), 0),
        "primal_start": scatter_about(seeds[7], (COLS,), 1.0, 4.0, ((0, 8),), jnp.float32),
        "dual_start": jnp.clip(1.0 * jax.random.uniform(seeds[8], (ROWS,), jnp.float32) ** block_levels(seeds[8], (ROWS,), ((0, 4),), -0.2, 0.2), 0.0, 1.0),
        "step_size": jnp.clip(jax.random.uniform(seeds[9], (1,), jnp.float32, 0.02, 0.06), 0.02, 0.06),
    }


EPSILON = 1e-06
HIGHEST = lax.Precision.HIGHEST

def reference(tile_values, tile_coords, tile_count, objective, lower, upper, rhs, primal_start, dual_start, step_size):
    group_tiles = N_COL * TILES_DEV
    row_total = N_ROW * RB_DEV
    col_total = N_COL * CB_DEV
    slots = jnp.arange(TILES_DEV, dtype=jnp.int32)
    in_use = (slots[None, None, :] < tile_count[:, :, None]).astype(jnp.float32)
    global_rows = (jnp.arange(N_ROW, dtype=jnp.int32)[:, None, None] * RB_DEV + tile_coords[..., 0]).astype(jnp.int32)
    global_cols = (jnp.arange(N_COL, dtype=jnp.int32)[None, :, None] * CB_DEV + tile_coords[..., 1]).astype(jnp.int32)
    groups = (tile_values.reshape(N_ROW, group_tiles, TILE, TILE), global_rows.reshape(N_ROW, group_tiles), global_cols.reshape(N_ROW, group_tiles), in_use.reshape(N_ROW, group_tiles))
    flat_rows = global_rows.reshape(-1)
    flat_cols = global_cols.reshape(-1)
    row_scale = jnp.ones((row_total, TILE), jnp.float32)
    col_scale = jnp.ones((col_total, TILE), jnp.float32)
    for sweep in range(RUIZ):

        def peaks(group, row_scale=row_scale, col_scale=col_scale):
            values, row_index, col_index, used = group
            magnitude = jnp.abs(values) * used[:, None, None]
            row_local = lax.optimization_barrier(jnp.max(magnitude * col_scale[col_index][:, None, :], axis=2))
            col_local = lax.optimization_barrier(jnp.max(magnitude * row_scale[row_index][:, :, None], axis=1))
            return (row_local, col_local)
        row_local, col_local = lax.map(peaks, groups)
        row_peak = jnp.zeros((row_total, TILE), jnp.float32).at[flat_rows].max(row_local.reshape(-1, TILE))
        col_peak = jnp.zeros((col_total, TILE), jnp.float32).at[flat_cols].max(col_local.reshape(-1, TILE))
        row_scale = row_scale / jnp.sqrt(row_scale * row_peak + EPSILON)
        col_scale = col_scale / jnp.sqrt(col_scale * col_peak + EPSILON)

    def forward(vector):

        def partial_value(group):
            values, row_index, col_index, used = group
            products = jnp.einsum('tij,tj->ti', values, vector[col_index], precision=HIGHEST) * used[:, None]
            return jax.ops.segment_sum(products, row_index, num_segments=row_total)
        return lax.optimization_barrier(jnp.sum(lax.map(partial_value, groups), axis=0))

    def adjoint(vector):

        def partial_value(group):
            values, row_index, col_index, used = group
            products = jnp.einsum('tij,ti->tj', values, vector[row_index], precision=HIGHEST) * used[:, None]
            return jax.ops.segment_sum(products, col_index, num_segments=col_total)
        return lax.optimization_barrier(jnp.sum(lax.map(partial_value, groups), axis=0))
    cost = col_scale * objective.reshape(col_total, TILE)
    bound = row_scale * rhs.reshape(row_total, TILE)
    low_scaled = lower.reshape(col_total, TILE) / col_scale
    high_scaled = upper.reshape(col_total, TILE) / col_scale
    primal = primal_start.reshape(col_total, TILE) / col_scale
    dual = dual_start.reshape(row_total, TILE) / row_scale
    weight = jnp.sqrt(jnp.sum(cost * cost) + EPSILON) / jnp.sqrt(jnp.sum(bound * bound) + EPSILON)
    primal_step = step_size[0] / weight
    dual_step = step_size[0] * weight
    for iteration in range(ITERS):
        image = adjoint(row_scale * dual)
        moved = jnp.clip(primal - primal_step * (cost - col_scale * image), low_scaled, high_scaled)
        extra = 2.0 * moved - primal
        total = forward(col_scale * extra)
        dual = jnp.maximum(dual + dual_step * (bound - row_scale * total), 0.0)
        primal = moved
    return ((col_scale * primal).reshape(-1), (row_scale * dual).reshape(-1))
```

```python
import functools

import jax
import jax.numpy as jnp
from jax import lax
from jax.experimental import pallas as pl
from jax.experimental.pallas import tpu as pltpu
from jax.sharding import PartitionSpec as P

RUIZ = 2
ITERS = 2
EPSILON = 1e-06
GROUP = 8
F32 = jnp.float32
BF16 = jnp.bfloat16
MESH = pl.DeviceIdType.MESH


def dot(a, b, dims=(1, 0)):
    return lax.dot_general(a, b, (((dims[0],), (dims[1],)), ((), ())), preferred_element_type=F32)


def split2(v):
    high = v.astype(BF16)
    return high, (v - high.astype(F32)).astype(BF16)


def pick(onehot, v, dims=(1, 0)):
    high = v.astype(BF16)
    rest = v - high.astype(F32)
    mid = rest.astype(BF16)
    low = (rest - mid.astype(F32)).astype(BF16)
    return (dot(onehot, high, dims) + dot(onehot, mid, dims)) + dot(onehot, low, dims)


def kernel(
    n_row,
    n_col,
    link,
    values_hbm,
    coords_ref,
    count_ref,
    objective_ref,
    lower_ref,
    upper_ref,
    rhs_ref,
    primal_ref,
    dual_ref,
    step_ref,
    primal_out,
    dual_out,
    tiles,
    halves,
    row_local,
    col_local,
    col_pieces,
    row_columns,
    lhs_pieces,
    products,
    col_box,
    link_box,
    norm_box,
    dual_box,
    load_sem,
    col_send,
    col_recv,
    link_send,
    link_recv,
    norm_send,
    norm_recv,
    dual_send,
    dual_recv,
):
    slots, width = tiles.shape[0], tiles.shape[2]
    cb = objective_ref.shape[0]
    rb = rhs_ref.shape[0]
    periods = n_col // n_row
    link_base = rb - link
    my_row = lax.axis_index("row")
    my_col = lax.axis_index("col")
    is_period = lax.rem(my_col, n_row) == my_row
    my_period = my_col // n_row
    period_base = pl.multiple_of(my_period * cb, cb)
    groups = jnp.where(is_period, slots // GROUP, min(slots, cb) // GROUP)

    def load(g):
        part = pl.ds(pl.multiple_of(g * GROUP, GROUP), GROUP)
        return pltpu.make_async_copy(values_hbm.at[part], tiles.at[part], load_sem.at[g])

    def start_load(g, carry):
        load(g).start()
        return carry

    lax.fori_loop(0, groups, start_load, 0)

    barrier = pltpu.get_barrier_semaphore()
    for d in range(1, n_row):
        pl.semaphore_signal(
            barrier, inc=1, device_id={"row": lax.rem(my_row + d, n_row)}, device_id_type=MESH
        )
    for d in range(1, n_col):
        pl.semaphore_signal(
            barrier, inc=1, device_id={"col": lax.rem(my_col + d, n_col)}, device_id_type=MESH
        )

    def remote(box, send, recv, axis, target, index, source):
        return pltpu.make_async_remote_copy(
            src_ref=box.at[source],
            dst_ref=box.at[source],
            send_sem=send.at[index],
            recv_sem=recv.at[source],
            device_id={axis: target},
            device_id_type=MESH,
        )

    class Exchange:
        def __init__(self, box, send, recv, axis):
            self.n = n_row if axis == "row" else n_col
            self.me = my_row if axis == "row" else my_col
            self.args = (box, send, recv, axis)

        def start(self):
            for d in range(1, self.n):
                remote(*self.args, lax.rem(self.me + d, self.n), d, self.me).start()

        def finish(self):
            for d in range(1, self.n):
                other = lax.rem(self.me + self.n - d, self.n)
                remote(*self.args, other, d, other).wait_recv()
            for d in range(1, self.n):
                remote(*self.args, lax.rem(self.me + d, self.n), d, self.me).wait_send()

    def col_exchange(phase):
        return Exchange(col_box.at[phase], col_send.at[phase], col_recv.at[phase], "row")

    def link_exchange(phase):
        return Exchange(link_box.at[phase], link_send.at[phase], link_recv.at[phase], "col")

    norm_exchange = Exchange(norm_box, norm_send, norm_recv, "col")

    square = (slots, slots)
    lane = lax.broadcasted_iota(jnp.int32, square, 1)
    sublane = lax.broadcasted_iota(jnp.int32, square, 0)
    lane_f = lane.astype(F32)
    used = sublane < count_ref[0, 0]
    block_row = jnp.broadcast_to(coords_ref[:, 0:1], square)
    block_col = jnp.broadcast_to(coords_ref[:, 1:2], square)
    local_row = jnp.where(is_period, block_row - period_base, block_row - (link_base - cb))

    def layout(place):
        place = jnp.where(used, place, 2 * slots - 1)
        onehot = jnp.where(place == lane, 1.0, 0.0)
        place_f = place.astype(F32)
        key = place_f * slots + sublane.astype(F32)
        rank = jnp.sum(jnp.where(key.T < key, 1.0, 0.0), axis=1, keepdims=True)
        order = jnp.where(jnp.broadcast_to(rank, square) == lane_f, 1.0, 0.0).T
        placed = jnp.broadcast_to(jnp.sum(order * place_f.T, axis=1, keepdims=True), square)
        masks = []
        d = 1
        while d < slots:
            masks.append(jnp.where(pltpu.roll(placed, slots - d, axis=0) == placed, 1.0, 0.0))
            d *= 2
        first = (pltpu.roll(placed, 1, axis=0) != placed) | (sublane == 0)
        head = jnp.where((placed == lane_f) & first, 1.0, 0.0).T
        return onehot.astype(BF16), onehot.T.astype(BF16), order.astype(BF16), masks, head.astype(BF16)

    row_pick, row_sum, row_order, row_masks, row_head = layout(local_row)
    col_pick, col_sum, col_order, col_masks, col_head = layout(block_col)

    def segment_max(ordered, masks, head):
        d = 1
        for mask in masks:
            ordered = jnp.maximum(ordered, mask * pltpu.roll(ordered, slots - d, axis=0))
            d *= 2
        return pick(head, ordered)

    row_local[...] = jnp.zeros_like(row_local)
    col_local[...] = jnp.zeros_like(col_local)
    products[...] = jnp.zeros_like(products)
    tile_lane = lax.broadcasted_iota(jnp.int32, (width, slots), 1)

    def first_peaks(g, carry):
        load(g).wait()
        joined = row_local[...]
        for k in range(GROUP):
            t = g * GROUP + k
            tile = tiles[t]
            high, low = split2(tile)
            halves[t, 0:width, :] = high
            halves[t, width : 2 * width, :] = low
            size = jnp.abs(tile)
            col_local[pl.ds(t, 1), :] = jnp.max(size, axis=0, keepdims=True)
            joined = jnp.where(tile_lane == t, jnp.max(size, axis=1, keepdims=True), joined)
        row_local[...] = joined
        return carry

    def next_peaks(g, carry):
        joined = row_local[...]
        columns = row_columns[g]
        for k in range(GROUP):
            t = g * GROUP + k
            size = jnp.abs(tiles[t])
            by_row = size * columns[:, k : k + 1]
            by_col = size * col_pieces[pl.ds(t, 1), :]
            col_local[pl.ds(t, 1), :] = jnp.max(by_row, axis=0, keepdims=True)
            joined = jnp.where(tile_lane == t, jnp.max(by_col, axis=1, keepdims=True), joined)
        row_local[...] = joined
        return carry

    def pad_rows(v):
        return jnp.concatenate([v, jnp.zeros((slots - v.shape[0], width), F32)], axis=0)

    row_scale = jnp.ones((slots, width), F32)
    col_scale = jnp.ones((cb, width), F32)
    for sweep in range(RUIZ):
        if sweep == 0:
            lax.fori_loop(0, groups, first_peaks, 0)
            pl.semaphore_wait(barrier, n_row + n_col - 2)
        else:
            col_pieces[...] = pick(col_pick, pad_rows(col_scale))
            turned = pick(row_pick, row_scale).T
            for g in range(slots // GROUP):
                row_columns[g] = turned[:, g * GROUP : (g + 1) * GROUP]
            lax.fori_loop(0, groups, next_peaks, 0)
        row_peak = segment_max(pick(row_order, row_local[...], (1, 1)), row_masks, row_head)
        col_peak = segment_max(pick(col_order, col_local[...]), col_masks, col_head)
        col_box[sweep, my_row, 0:cb, :] = col_peak[0:cb]
        link_box[sweep, my_col] = row_peak[cb : cb + link]
        col_exchange(sweep).start()
        link_exchange(sweep).start()
        col_exchange(sweep).finish()
        link_exchange(sweep).finish()
        link_peak = functools.reduce(jnp.maximum, [link_box[sweep, c] for c in range(n_col)])
        col_peak = functools.reduce(jnp.maximum, [col_box[sweep, r, 0:cb, :] for r in range(n_row)])
        row_peak = jnp.concatenate([row_peak[0:cb], link_peak, row_peak[cb + link :]], axis=0)
        row_scale = row_scale / jnp.sqrt(row_scale * row_peak + EPSILON)
        col_scale = col_scale / jnp.sqrt(col_scale * col_peak + EPSILON)

    def local_rows(ref):
        return pad_rows(jnp.concatenate([ref[pl.ds(period_base, cb), :], ref[link_base:rb, :]], axis=0))

    cost = col_scale * objective_ref[...]
    bound = row_scale * local_rows(rhs_ref)
    low_scaled = lower_ref[...] / col_scale
    high_scaled = upper_ref[...] / col_scale
    primal = primal_ref[...] / col_scale
    dual = local_rows(dual_ref) / row_scale

    def fold(v):
        return jnp.sum(v.reshape(v.shape[0] // 8, 8, width), axis=0)

    norm_box[my_col, 0:8, :] = fold(cost * cost)
    norm_box[my_col, 8:16, :] = jnp.where(is_period, fold(bound[0:cb] * bound[0:cb]), 0.0)
    norm_exchange.start()

    def put_pieces(onehot, v):
        high, low = split2(v)
        shape = (slots // GROUP, GROUP, width)
        lhs_pieces[...] = jnp.concatenate(
            [dot(onehot, high).reshape(shape), dot(onehot, low).reshape(shape)], axis=1
        ).astype(BF16)

    pair_row = lax.rem(lax.broadcasted_iota(jnp.int32, (2 * GROUP, width), 0), GROUP)

    def adjoint_step(g, carry):
        lhs = lhs_pieces[g]
        both = jnp.concatenate([lhs, lhs], axis=1)
        joined = jnp.zeros((2 * GROUP, width), F32)
        for k in range(GROUP):
            joined = jnp.where(pair_row == k, dot(both, halves[g * GROUP + k]), joined)
        part = pl.ds(pl.multiple_of(g * GROUP, GROUP), GROUP)
        products[part, :] = joined[0:GROUP] + joined[GROUP:]
        return carry

    def forward_step(g, carry):
        lhs = lhs_pieces[g]
        joined = jnp.zeros((2 * GROUP, width), F32)
        for k in range(GROUP):
            pair = dot(lhs, halves[g * GROUP + k], (1, 1))
            joined = jnp.where(pair_row == k, pair[:, 0:width] + pair[:, width:], joined)
        part = pl.ds(pl.multiple_of(g * GROUP, GROUP), GROUP)
        products[part, :] = joined[0:GROUP] + joined[GROUP:]
        return carry

    for iteration in range(ITERS):
        phase = RUIZ + iteration
        put_pieces(row_pick, row_scale * dual)
        lax.fori_loop(0, groups, adjoint_step, 0)
        col_box[phase, my_row, 0:cb, :] = pick(col_sum, products[...])[0:cb]
        if iteration == 0:
            norm_exchange.finish()
            cost_sum = functools.reduce(jnp.add, [norm_box[c, 0:8, :] for c in range(n_col)])
            bound_sum = functools.reduce(jnp.add, [norm_box[c, 8:16, :] for c in range(n_col)])
            link_bound = bound[cb : cb + link]
            col_box[phase, my_row, cb : cb + 8, :] = bound_sum + fold(link_bound * link_bound)
        col_exchange(phase).start()
        col_exchange(phase).finish()
        image = functools.reduce(jnp.add, [col_box[phase, r, 0:cb, :] for r in range(n_row)])
        if iteration == 0:
            bound_sum = functools.reduce(
                jnp.add, [col_box[phase, r, cb : cb + 8, :] for r in range(n_row)]
            )
            cost_total = jnp.sum(cost_sum, keepdims=True)
            bound_total = jnp.sum(bound_sum, keepdims=True)
            weight = jnp.sqrt(cost_total + EPSILON) / jnp.sqrt(bound_total + EPSILON)
            primal_step = step_ref[0] / weight
            dual_step = step_ref[0] * weight
        moved = jnp.clip(primal - primal_step * (cost - col_scale * image), low_scaled, high_scaled)
        put_pieces(col_pick, pad_rows(col_scale * (2.0 * moved - primal)))
        lax.fori_loop(0, groups, forward_step, 0)
        total = pick(row_sum, products[...])
        link_box[phase, my_col] = total[cb : cb + link]
        link_exchange(phase).start()
        primal = moved
        own = jnp.maximum(
            dual[0:cb] + dual_step * (bound[0:cb] - row_scale[0:cb] * total[0:cb]), 0.0
        )
        if iteration == ITERS - 1:

            @pl.when(is_period)
            def _():
                dual_box[my_period] = row_scale[0:cb] * own
                for d in range(1, n_col):
                    pltpu.make_async_remote_copy(
                        src_ref=dual_box.at[my_period],
                        dst_ref=dual_box.at[my_period],
                        send_sem=dual_send.at[d],
                        recv_sem=dual_recv.at[my_period],
                        device_id={"col": lax.rem(my_col + d, n_col)},
                        device_id_type=MESH,
                    ).start()

            primal_out[...] = col_scale * primal
        link_exchange(phase).finish()
        link_total = functools.reduce(jnp.add, [link_box[phase, c] for c in range(n_col)])
        span = slice(cb, cb + link)
        link_dual = jnp.maximum(
            dual[span] + dual_step * (bound[span] - row_scale[span] * link_total), 0.0
        )
        dual = pad_rows(jnp.concatenate([own, link_dual], axis=0))
    dual_out[link_base:rb, :] = (row_scale * dual)[cb : cb + link]
    for p in range(periods):
        owner = p * n_row + my_row

        @pl.when(owner != my_col)
        def _():
            pltpu.make_async_remote_copy(
                src_ref=dual_box.at[p],
                dst_ref=dual_box.at[p],
                send_sem=dual_send.at[0],
                recv_sem=dual_recv.at[p],
                device_id={"col": lax.rem(my_col + 1, n_col)},
                device_id_type=MESH,
            ).wait_recv()

        dual_out[p * cb : (p + 1) * cb, :] = dual_box[p]

    @pl.when(is_period)
    def _():
        for d in range(1, n_col):
            pltpu.make_async_remote_copy(
                src_ref=dual_box.at[my_period],
                dst_ref=dual_box.at[my_period],
                send_sem=dual_send.at[d],
                recv_sem=dual_recv.at[my_period],
                device_id={"col": lax.rem(my_col + d, n_col)},
                device_id_type=MESH,
            ).wait_send()


def local(
    n_row,
    n_col,
    tile_values,
    tile_coords,
    tile_count,
    objective,
    lower,
    upper,
    rhs,
    primal_start,
    dual_start,
    step_size,
):
    width = tile_values.shape[-1]
    slots = tile_values.shape[2]
    cb = objective.shape[0] // width
    rb = rhs.shape[0] // width
    periods = n_col // n_row
    link = rb - periods * cb
    vmem = pl.BlockSpec(memory_space=pltpu.VMEM)
    smem = pl.BlockSpec(memory_space=pltpu.SMEM)
    phases = RUIZ + ITERS
    dma = pltpu.SemaphoreType.DMA
    primal, dual = pl.pallas_call(
        functools.partial(kernel, n_row, n_col, link),
        out_shape=(
            jax.ShapeDtypeStruct((cb, width), F32),
            jax.ShapeDtypeStruct((rb, width), F32),
        ),
        in_specs=[pl.BlockSpec(memory_space=pl.ANY), vmem, smem] + [vmem] * 6 + [smem],
        out_specs=(vmem, vmem),
        scratch_shapes=[
            pltpu.VMEM((slots, width, width), F32),
            pltpu.VMEM((slots, 2 * width, width), BF16),
            pltpu.VMEM((width, slots), F32),
            pltpu.VMEM((slots, width), F32),
            pltpu.VMEM((slots, width), F32),
            pltpu.VMEM((slots // GROUP, width, GROUP), F32),
            pltpu.VMEM((slots // GROUP, 2 * GROUP, width), BF16),
            pltpu.VMEM((slots, width), F32),
            pltpu.VMEM((phases, n_row, cb + 8, width), F32),
            pltpu.VMEM((phases, n_col, link, width), F32),
            pltpu.VMEM((n_col, 16, width), F32),
            pltpu.VMEM((periods, cb, width), F32),
            dma((slots // GROUP,)),
            dma((phases, n_row)),
            dma((phases, n_row)),
            dma((phases, n_col)),
            dma((phases, n_col)),
            dma((n_col,)),
            dma((n_col,)),
            dma((n_col,)),
            dma((periods,)),
        ],
        compiler_params=pltpu.CompilerParams(
            collective_id=0, has_side_effects=True, vmem_limit_bytes=40 * 1024 * 1024
        ),
        name="ruiz_pdhg",
    )(
        tile_values.reshape(slots, width, width),
        tile_coords.reshape(slots, 2),
        tile_count.reshape(1, 1),
        objective.reshape(cb, width),
        lower.reshape(cb, width),
        upper.reshape(cb, width),
        rhs.reshape(rb, width),
        primal_start.reshape(cb, width),
        dual_start.reshape(rb, width),
        step_size,
    )
    return primal.reshape(-1), dual.reshape(-1)


def solution(mesh):
    placed = (
        P("row", "col", None, None, None),
        P("row", "col", None, None),
        P("row", "col"),
        P("col"),
        P("col"),
        P("col"),
        P("row"),
        P("col"),
        P("row"),
        P(),
    )
    return jax.shard_map(
        functools.partial(local, mesh.shape["row"], mesh.shape["col"]),
        mesh=mesh,
        in_specs=placed,
        out_specs=(P("col"), P("row")),
        check_vma=False,
    )
```

```python
import functools

import jax
import jax.numpy as jnp
from jax import lax
from jax.experimental import pallas as pl
from jax.experimental.pallas import tpu as pltpu
from jax.sharding import PartitionSpec as P

RUIZ = 2
ITERS = 2
EPSILON = 1e-06
GROUP = 8
F32 = jnp.float32
BF16 = jnp.bfloat16
MESH = pl.DeviceIdType.MESH


def dot(a, b, dims=(1, 0)):
    return lax.dot_general(a, b, (((dims[0],), (dims[1],)), ((), ())), preferred_element_type=F32)


def split2(v):
    high = v.astype(BF16)
    return high, (v - high.astype(F32)).astype(BF16)


def pick(onehot, v, dims=(1, 0)):
    high = v.astype(BF16)
    rest = v - high.astype(F32)
    mid = rest.astype(BF16)
    low = (rest - mid.astype(F32)).astype(BF16)
    return (dot(onehot, high, dims) + dot(onehot, mid, dims)) + dot(onehot, low, dims)


def kernel(
    n_row,
    n_col,
    link,
    values_hbm,
    coords_ref,
    count_ref,
    objective_ref,
    lower_ref,
    upper_ref,
    rhs_ref,
    primal_ref,
    dual_ref,
    step_ref,
    primal_out,
    dual_out,
    tiles,
    halves,
    row_local,
    col_local,
    col_pieces,
    turned,
    lhs_pieces,
    products,
    col_box,
    link_box,
    norm_box,
    dual_box,
    load_sem,
    col_send,
    col_recv,
    link_send,
    link_recv,
    norm_send,
    norm_recv,
    dual_send,
    dual_recv,
):
    slots, width = tiles.shape[0], tiles.shape[2]
    cb = objective_ref.shape[0]
    rb = rhs_ref.shape[0]
    periods = n_col // n_row
    link_base = rb - link
    my_row = lax.axis_index("row")
    my_col = lax.axis_index("col")
    is_period = lax.rem(my_col, n_row) == my_row
    my_period = my_col // n_row
    period_base = pl.multiple_of(my_period * cb, cb)
    groups = jnp.where(is_period, slots // GROUP, min(slots, cb) // GROUP)

    def load(g):
        part = pl.ds(pl.multiple_of(g * GROUP, GROUP), GROUP)
        return pltpu.make_async_copy(values_hbm.at[part], tiles.at[part], load_sem.at[g])

    def start_load(g, carry):
        load(g).start()
        return carry

    lax.fori_loop(0, groups, start_load, 0)

    barrier = pltpu.get_barrier_semaphore()
    for d in range(1, n_row):
        pl.semaphore_signal(
            barrier, inc=1, device_id={"row": lax.rem(my_row + d, n_row)}, device_id_type=MESH
        )
    for d in range(1, n_col):
        pl.semaphore_signal(
            barrier, inc=1, device_id={"col": lax.rem(my_col + d, n_col)}, device_id_type=MESH
        )

    def remote(box, send, recv, axis, target, index, source):
        return pltpu.make_async_remote_copy(
            src_ref=box.at[source],
            dst_ref=box.at[source],
            send_sem=send.at[index],
            recv_sem=recv.at[source],
            device_id={axis: target},
            device_id_type=MESH,
        )

    class Exchange:
        def __init__(self, box, send, recv, axis):
            self.n = n_row if axis == "row" else n_col
            self.me = my_row if axis == "row" else my_col
            self.args = (box, send, recv, axis)

        def start(self):
            for d in range(1, self.n):
                remote(*self.args, lax.rem(self.me + d, self.n), d, self.me).start()

        def finish(self):
            for d in range(1, self.n):
                other = lax.rem(self.me + self.n - d, self.n)
                remote(*self.args, other, d, other).wait_recv()
            for d in range(1, self.n):
                remote(*self.args, lax.rem(self.me + d, self.n), d, self.me).wait_send()

    def col_exchange(phase):
        return Exchange(col_box.at[phase], col_send.at[phase], col_recv.at[phase], "row")

    def link_exchange(phase):
        return Exchange(link_box.at[phase], link_send.at[phase], link_recv.at[phase], "col")

    norm_exchange = Exchange(norm_box, norm_send, norm_recv, "col")

    square = (slots, slots)
    lane = lax.broadcasted_iota(jnp.int32, square, 1)
    sublane = lax.broadcasted_iota(jnp.int32, square, 0)
    lane_f = lane.astype(F32)
    used = sublane < count_ref[0, 0]
    block_row = jnp.broadcast_to(coords_ref[:, 0:1], square)
    block_col = jnp.broadcast_to(coords_ref[:, 1:2], square)
    local_row = jnp.where(is_period, block_row - period_base, block_row - (link_base - cb))

    def layout(place):
        place = jnp.where(used, place, 2 * slots - 1)
        onehot = jnp.where(place == lane, 1.0, 0.0)
        place_f = place.astype(F32)
        key = place_f * slots + sublane.astype(F32)
        rank = jnp.sum(jnp.where(key.T < key, 1.0, 0.0), axis=1, keepdims=True)
        order = jnp.where(jnp.broadcast_to(rank, square) == lane_f, 1.0, 0.0).T
        placed = jnp.broadcast_to(jnp.sum(order * place_f.T, axis=1, keepdims=True), square)
        masks = []
        d = 1
        while d < slots:
            masks.append(jnp.where(pltpu.roll(placed, slots - d, axis=0) == placed, 1.0, 0.0))
            d *= 2
        first = (pltpu.roll(placed, 1, axis=0) != placed) | (sublane == 0)
        head = jnp.where((placed == lane_f) & first, 1.0, 0.0).T
        return onehot.astype(BF16), onehot.T.astype(BF16), order.astype(BF16), masks, head.astype(BF16)

    row_pick, row_sum, row_order, row_masks, row_head = layout(local_row)
    col_pick, col_sum, col_order, col_masks, col_head = layout(block_col)

    def segment_max(ordered, masks, head):
        d = 1
        for mask in masks:
            ordered = jnp.maximum(ordered, mask * pltpu.roll(ordered, slots - d, axis=0))
            d *= 2
        return pick(head, ordered)

    row_local[...] = jnp.zeros_like(row_local)
    col_local[...] = jnp.zeros_like(col_local)
    products[...] = jnp.zeros_like(products)
    tile_lane = lax.broadcasted_iota(jnp.int32, (width, slots), 1)

    def first_peaks(g, carry):
        load(g).wait()
        joined = row_local[...]
        for k in range(GROUP):
            t = g * GROUP + k
            tile = tiles[t]
            size = jnp.abs(tile)
            col_local[pl.ds(t, 1), :] = jnp.max(size, axis=0, keepdims=True)
            joined = jnp.where(tile_lane == t, jnp.max(size, axis=1, keepdims=True), joined)
        row_local[...] = joined
        return carry

    spread_shape = (2 * GROUP, GROUP * width)
    spread = jnp.where(
        lax.rem(lax.broadcasted_iota(jnp.int32, spread_shape, 0), GROUP)
        == lax.div(lax.broadcasted_iota(jnp.int32, spread_shape, 1), width),
        1.0,
        0.0,
    ).astype(BF16)

    def next_col_peaks(g, carry):
        columns = dot(lhs_pieces[g], spread, (0, 0))
        for k in range(GROUP):
            t = g * GROUP + k
            by_row = jnp.abs(tiles[t]) * columns[:, k * width : (k + 1) * width]
            col_local[pl.ds(t, 1), :] = jnp.max(by_row, axis=0, keepdims=True)
        return carry

    def next_row_peaks(g, carry):
        joined = row_local[...]
        for k in range(GROUP):
            t = g * GROUP + k
            by_col = jnp.abs(tiles[t]) * col_pieces[pl.ds(t, 1), :]
            joined = jnp.where(tile_lane == t, jnp.max(by_col, axis=1, keepdims=True), joined)
        row_local[...] = joined
        return carry

    def keep_halves(g, carry):
        for k in range(GROUP):
            t = g * GROUP + k
            halves[t, 0:width, :], halves[t, width : 2 * width, :] = split2(tiles[t])
        return carry

    def keep_turned(g, carry):
        for k in range(GROUP):
            t = g * GROUP + k
            turned[t, 0:width, :], turned[t, width : 2 * width, :] = split2(tiles[t].T)
        return carry

    def put_pieces(onehot, v):
        high, low = split2(v)
        shape = (slots // GROUP, GROUP, width)
        lhs_pieces[...] = jnp.concatenate(
            [dot(onehot, high).reshape(shape), dot(onehot, low).reshape(shape)], axis=1
        ).astype(BF16)

    def pad_rows(v):
        return jnp.concatenate([v, jnp.zeros((slots - v.shape[0], width), F32)], axis=0)

    row_scale = jnp.ones((slots, width), F32)
    col_scale = jnp.ones((cb, width), F32)
    for sweep in range(RUIZ):
        if sweep == 0:
            lax.fori_loop(0, groups, first_peaks, 0)
            pl.semaphore_wait(barrier, n_row + n_col - 2)
        else:
            col_pieces[...] = pick(col_pick, pad_rows(col_scale))

            @pl.when(jnp.logical_not(is_period))
            def _():
                put_pieces(row_pick, row_scale)
                lax.fori_loop(0, groups, next_col_peaks, 0)

            lax.fori_loop(0, groups, next_row_peaks, 0)
        row_peak = segment_max(pick(row_order, row_local[...], (1, 1)), row_masks, row_head)
        col_peak = segment_max(pick(col_order, col_local[...]), col_masks, col_head)
        col_box[sweep, my_row, 0:cb, :] = col_peak[0:cb]
        link_box[sweep, my_col] = row_peak[cb : cb + link]
        col_exchange(sweep).start()
        link_exchange(sweep).start()
        if sweep == 0:
            @pl.when(is_period)
            def _():
                put_pieces(row_pick, row_scale / jnp.sqrt(row_scale * row_peak + EPSILON))
                lax.fori_loop(0, groups, next_col_peaks, 0)

            lax.fori_loop(0, groups, keep_halves, 0)
        else:
            lax.fori_loop(0, groups, keep_turned, 0)
        col_exchange(sweep).finish()
        link_exchange(sweep).finish()
        link_peak = functools.reduce(jnp.maximum, [link_box[sweep, c] for c in range(n_col)])
        col_peak = functools.reduce(jnp.maximum, [col_box[sweep, r, 0:cb, :] for r in range(n_row)])
        row_peak = jnp.concatenate([row_peak[0:cb], link_peak, row_peak[cb + link :]], axis=0)
        row_scale = row_scale / jnp.sqrt(row_scale * row_peak + EPSILON)
        col_scale = col_scale / jnp.sqrt(col_scale * col_peak + EPSILON)

    def local_rows(ref):
        return pad_rows(jnp.concatenate([ref[pl.ds(period_base, cb), :], ref[link_base:rb, :]], axis=0))

    cost = col_scale * objective_ref[...]
    bound = row_scale * local_rows(rhs_ref)
    low_scaled = lower_ref[...] / col_scale
    high_scaled = upper_ref[...] / col_scale
    primal = primal_ref[...] / col_scale
    dual = local_rows(dual_ref) / row_scale

    def fold(v):
        return jnp.sum(v.reshape(v.shape[0] // 8, 8, width), axis=0)

    norm_box[my_col, 0:8, :] = fold(cost * cost)
    norm_box[my_col, 8:16, :] = jnp.where(is_period, fold(bound[0:cb] * bound[0:cb]), 0.0)
    norm_exchange.start()

    pair_row = lax.rem(lax.broadcasted_iota(jnp.int32, (2 * GROUP, width), 0), GROUP)

    def product_step(weights, g, carry):
        lhs = lhs_pieces[g]
        both = jnp.concatenate([lhs, lhs], axis=1)
        joined = jnp.zeros((2 * GROUP, width), F32)
        for k in range(GROUP):
            joined = jnp.where(pair_row == k, dot(both, weights[g * GROUP + k]), joined)
        part = pl.ds(pl.multiple_of(g * GROUP, GROUP), GROUP)
        products[part, :] = joined[0:GROUP] + joined[GROUP:]
        return carry

    for iteration in range(ITERS):
        phase = RUIZ + iteration
        put_pieces(row_pick, row_scale * dual)
        lax.fori_loop(0, groups, functools.partial(product_step, halves), 0)
        col_box[phase, my_row, 0:cb, :] = pick(col_sum, products[...])[0:cb]
        if iteration == 0:
            norm_exchange.finish()
            cost_sum = functools.reduce(jnp.add, [norm_box[c, 0:8, :] for c in range(n_col)])
            bound_sum = functools.reduce(jnp.add, [norm_box[c, 8:16, :] for c in range(n_col)])
            link_bound = bound[cb : cb + link]
            col_box[phase, my_row, cb : cb + 8, :] = bound_sum + fold(link_bound * link_bound)
        col_exchange(phase).start()
        col_exchange(phase).finish()
        image = functools.reduce(jnp.add, [col_box[phase, r, 0:cb, :] for r in range(n_row)])
        if iteration == 0:
            bound_sum = functools.reduce(
                jnp.add, [col_box[phase, r, cb : cb + 8, :] for r in range(n_row)]
            )
            cost_total = jnp.sum(cost_sum, keepdims=True)
            bound_total = jnp.sum(bound_sum, keepdims=True)
            weight = jnp.sqrt(cost_total + EPSILON) / jnp.sqrt(bound_total + EPSILON)
            primal_step = step_ref[0] / weight
            dual_step = step_ref[0] * weight
        moved = jnp.clip(primal - primal_step * (cost - col_scale * image), low_scaled, high_scaled)
        put_pieces(col_pick, pad_rows(col_scale * (2.0 * moved - primal)))
        lax.fori_loop(0, groups, functools.partial(product_step, turned), 0)
        total = pick(row_sum, products[...])
        link_box[phase, my_col] = total[cb : cb + link]
        link_exchange(phase).start()
        primal = moved
        own = jnp.maximum(
            dual[0:cb] + dual_step * (bound[0:cb] - row_scale[0:cb] * total[0:cb]), 0.0
        )
        if iteration == ITERS - 1:

            @pl.when(is_period)
            def _():
                dual_box[my_period] = row_scale[0:cb] * own
                for d in range(1, n_col):
                    pltpu.make_async_remote_copy(
                        src_ref=dual_box.at[my_period],
                        dst_ref=dual_box.at[my_period],
                        send_sem=dual_send.at[d],
                        recv_sem=dual_recv.at[my_period],
                        device_id={"col": lax.rem(my_col + d, n_col)},
                        device_id_type=MESH,
                    ).start()

            primal_out[...] = col_scale * primal
        link_exchange(phase).finish()
        link_total = functools.reduce(jnp.add, [link_box[phase, c] for c in range(n_col)])
        span = slice(cb, cb + link)
        link_dual = jnp.maximum(
            dual[span] + dual_step * (bound[span] - row_scale[span] * link_total), 0.0
        )
        dual = pad_rows(jnp.concatenate([own, link_dual], axis=0))
    dual_out[link_base:rb, :] = (row_scale * dual)[cb : cb + link]
    for p in range(periods):
        owner = p * n_row + my_row

        @pl.when(owner != my_col)
        def _():
            pltpu.make_async_remote_copy(
                src_ref=dual_box.at[p],
                dst_ref=dual_box.at[p],
                send_sem=dual_send.at[0],
                recv_sem=dual_recv.at[p],
                device_id={"col": lax.rem(my_col + 1, n_col)},
                device_id_type=MESH,
            ).wait_recv()

        dual_out[p * cb : (p + 1) * cb, :] = dual_box[p]

    @pl.when(is_period)
    def _():
        for d in range(1, n_col):
            pltpu.make_async_remote_copy(
                src_ref=dual_box.at[my_period],
                dst_ref=dual_box.at[my_period],
                send_sem=dual_send.at[d],
                recv_sem=dual_recv.at[my_period],
                device_id={"col": lax.rem(my_col + d, n_col)},
                device_id_type=MESH,
            ).wait_send()


def local(
    n_row,
    n_col,
    tile_values,
    tile_coords,
    tile_count,
    objective,
    lower,
    upper,
    rhs,
    primal_start,
    dual_start,
    step_size,
):
    width = tile_values.shape[-1]
    slots = tile_values.shape[2]
    cb = objective.shape[0] // width
    rb = rhs.shape[0] // width
    periods = n_col // n_row
    link = rb - periods * cb
    vmem = pl.BlockSpec(memory_space=pltpu.VMEM)
    smem = pl.BlockSpec(memory_space=pltpu.SMEM)
    phases = RUIZ + ITERS
    dma = pltpu.SemaphoreType.DMA
    primal, dual = pl.pallas_call(
        functools.partial(kernel, n_row, n_col, link),
        out_shape=(
            jax.ShapeDtypeStruct((cb, width), F32),
            jax.ShapeDtypeStruct((rb, width), F32),
        ),
        in_specs=[pl.BlockSpec(memory_space=pl.ANY), vmem, smem] + [vmem] * 6 + [smem],
        out_specs=(vmem, vmem),
        scratch_shapes=[
            pltpu.VMEM((slots, width, width), F32),
            pltpu.VMEM((slots, 2 * width, width), BF16),
            pltpu.VMEM((width, slots), F32),
            pltpu.VMEM((slots, width), F32),
            pltpu.VMEM((slots, width), F32),
            pltpu.VMEM((slots, 2 * width, width), BF16),
            pltpu.VMEM((slots // GROUP, 2 * GROUP, width), BF16),
            pltpu.VMEM((slots, width), F32),
            pltpu.VMEM((phases, n_row, cb + 8, width), F32),
            pltpu.VMEM((phases, n_col, link, width), F32),
            pltpu.VMEM((n_col, 16, width), F32),
            pltpu.VMEM((periods, cb, width), F32),
            dma((slots // GROUP,)),
            dma((phases, n_row)),
            dma((phases, n_row)),
            dma((phases, n_col)),
            dma((phases, n_col)),
            dma((n_col,)),
            dma((n_col,)),
            dma((n_col,)),
            dma((periods,)),
        ],
        compiler_params=pltpu.CompilerParams(
            collective_id=0, has_side_effects=True, vmem_limit_bytes=48 * 1024 * 1024
        ),
        name="ruiz_pdhg",
    )(
        tile_values.reshape(slots, width, width),
        tile_coords.reshape(slots, 2),
        tile_count.reshape(1, 1),
        objective.reshape(cb, width),
        lower.reshape(cb, width),
        upper.reshape(cb, width),
        rhs.reshape(rb, width),
        primal_start.reshape(cb, width),
        dual_start.reshape(rb, width),
        step_size,
    )
    return primal.reshape(-1), dual.reshape(-1)


def solution(mesh):
    placed = (
        P("row", "col", None, None, None),
        P("row", "col", None, None),
        P("row", "col"),
        P("col"),
        P("col"),
        P("col"),
        P("row"),
        P("col"),
        P("row"),
        P(),
    )
    return jax.shard_map(
        functools.partial(local, mesh.shape["row"], mesh.shape["col"]),
        mesh=mesh,
        in_specs=placed,
        out_specs=(P("col"), P("row")),
        check_vma=False,
    )
```

```python
import functools

import jax
import jax.numpy as jnp
from jax import lax
from jax.experimental import pallas as pl
from jax.experimental.pallas import tpu as pltpu
from jax.sharding import PartitionSpec as P

RUIZ = 2
ITERS = 2
EPSILON = 1e-06
GROUP = 8
F32 = jnp.float32
BF16 = jnp.bfloat16
MESH = pl.DeviceIdType.MESH


def dot(a, b, dims=(1, 0)):
    return lax.dot_general(a, b, (((dims[0],), (dims[1],)), ((), ())), preferred_element_type=F32)


def split2(v):
    high = v.astype(BF16)
    return high, (v - high.astype(F32)).astype(BF16)


def pick(onehot, v, dims=(1, 0)):
    high = v.astype(BF16)
    rest = v - high.astype(F32)
    mid = rest.astype(BF16)
    low = (rest - mid.astype(F32)).astype(BF16)
    return (dot(onehot, high, dims) + dot(onehot, mid, dims)) + dot(onehot, low, dims)


def kernel(
    n_row,
    n_col,
    link,
    values_hbm,
    coords_hbm,
    count_ref,
    objective_hbm,
    lower_hbm,
    upper_hbm,
    rhs_hbm,
    primal_hbm,
    dual_hbm,
    step_ref,
    primal_out,
    dual_out,
    tiles,
    halves,
    row_local,
    col_local,
    col_pieces,
    turned,
    lhs_pieces,
    products,
    col_box,
    link_box,
    norm_box,
    dual_box,
    coords_ref,
    objective_ref,
    lower_ref,
    upper_ref,
    rhs_ref,
    primal_ref,
    dual_ref,
    input_sem,
    load_sem,
    col_send,
    col_recv,
    link_send,
    link_recv,
    norm_send,
    norm_recv,
    dual_send,
    dual_recv,
):
    slots, width = tiles.shape[0], tiles.shape[2]
    cb = objective_ref.shape[0]
    rb = rhs_ref.shape[0]
    periods = n_col // n_row
    link_base = rb - link
    my_row = lax.axis_index("row")
    my_col = lax.axis_index("col")
    is_period = lax.rem(my_col, n_row) == my_row
    my_period = my_col // n_row
    period_base = pl.multiple_of(my_period * cb, cb)
    groups = jnp.where(is_period, slots // GROUP, min(slots, cb) // GROUP)

    staged = [
        pltpu.make_async_copy(source, target, input_sem.at[i])
        for i, (source, target) in enumerate(
            (
                (coords_hbm, coords_ref),
                (objective_hbm, objective_ref),
                (lower_hbm, lower_ref),
                (upper_hbm, upper_ref),
                (rhs_hbm, rhs_ref),
                (primal_hbm, primal_ref),
                (dual_hbm, dual_ref),
            )
        )
    ]
    for copy in staged[:1]:
        copy.start()

    def load(g):
        part = pl.ds(pl.multiple_of(g * GROUP, GROUP), GROUP)
        return pltpu.make_async_copy(values_hbm.at[part], tiles.at[part], load_sem.at[g])

    def start_load(g, carry):
        load(g).start()
        return carry

    lax.fori_loop(0, groups, start_load, 0)
    for copy in staged[1:]:
        copy.start()

    barrier = pltpu.get_barrier_semaphore()
    for d in range(1, n_row):
        pl.semaphore_signal(
            barrier, inc=1, device_id={"row": lax.rem(my_row + d, n_row)}, device_id_type=MESH
        )
    for d in range(1, n_col):
        pl.semaphore_signal(
            barrier, inc=1, device_id={"col": lax.rem(my_col + d, n_col)}, device_id_type=MESH
        )

    def remote(box, send, recv, axis, target, index, source):
        return pltpu.make_async_remote_copy(
            src_ref=box.at[source],
            dst_ref=box.at[source],
            send_sem=send.at[index],
            recv_sem=recv.at[source],
            device_id={axis: target},
            device_id_type=MESH,
        )

    class Exchange:
        def __init__(self, box, send, recv, axis):
            self.n = n_row if axis == "row" else n_col
            self.me = my_row if axis == "row" else my_col
            self.args = (box, send, recv, axis)

        def start(self):
            for d in range(1, self.n):
                remote(*self.args, lax.rem(self.me + d, self.n), d, self.me).start()

        def finish(self):
            for d in range(1, self.n):
                other = lax.rem(self.me + self.n - d, self.n)
                remote(*self.args, other, d, other).wait_recv()

        def drain(self):
            for d in range(1, self.n):
                remote(*self.args, lax.rem(self.me + d, self.n), d, self.me).wait_send()

    def col_exchange(phase):
        return Exchange(col_box.at[phase], col_send.at[phase], col_recv.at[phase], "row")

    def link_exchange(phase):
        return Exchange(link_box.at[phase], link_send.at[phase], link_recv.at[phase], "col")

    norm_exchange = Exchange(norm_box, norm_send, norm_recv, "col")

    square = (slots, slots)
    lane = lax.broadcasted_iota(jnp.int32, square, 1)
    sublane = lax.broadcasted_iota(jnp.int32, square, 0)
    lane_f = lane.astype(F32)
    for copy in staged[:1]:
        copy.wait()
    used = sublane < count_ref[0, 0]
    coords = coords_ref[...].astype(F32)
    block_row = jnp.broadcast_to(coords[0:1, :], square).T.astype(jnp.int32)
    block_col = jnp.broadcast_to(coords[1:2, :], square).T.astype(jnp.int32)
    local_row = jnp.where(is_period, block_row - period_base, block_row - (link_base - cb))

    def layout(place):
        place = jnp.where(used, place, 2 * slots - 1)
        onehot = jnp.where(place == lane, 1.0, 0.0)
        place_f = place.astype(F32)
        key = place_f * slots + sublane.astype(F32)
        rank = jnp.sum(jnp.where(key.T < key, 1.0, 0.0), axis=1, keepdims=True)
        order = jnp.where(jnp.broadcast_to(rank, square) == lane_f, 1.0, 0.0).T
        placed = jnp.broadcast_to(jnp.sum(order * place_f.T, axis=1, keepdims=True), square)
        masks = []
        d = 1
        while d < slots:
            masks.append(jnp.where(pltpu.roll(placed, slots - d, axis=0) == placed, 1.0, 0.0))
            d *= 2
        first = (pltpu.roll(placed, 1, axis=0) != placed) | (sublane == 0)
        head = jnp.where((placed == lane_f) & first, 1.0, 0.0).T
        return onehot.astype(BF16), onehot.T.astype(BF16), order.astype(BF16), masks, head.astype(BF16)

    row_pick, row_sum, row_order, row_masks, row_head = layout(local_row)
    col_pick, col_sum, col_order, col_masks, col_head = layout(block_col)

    def segment_max(ordered, masks, head):
        d = 1
        for mask in masks:
            ordered = jnp.maximum(ordered, mask * pltpu.roll(ordered, slots - d, axis=0))
            d *= 2
        return pick(head, ordered)

    row_local[...] = jnp.zeros_like(row_local)
    col_local[...] = jnp.zeros_like(col_local)
    products[...] = jnp.zeros_like(products)
    tile_lane = lax.broadcasted_iota(jnp.int32, (width, slots), 1)

    def first_peaks(g, carry):
        load(g).wait()
        joined = row_local[...]
        for k in range(GROUP):
            t = g * GROUP + k
            tile = tiles[t]
            size = jnp.abs(tile)
            col_local[pl.ds(t, 1), :] = jnp.max(size, axis=0, keepdims=True)
            joined = jnp.where(tile_lane == t, jnp.max(size, axis=1, keepdims=True), joined)
        row_local[...] = joined
        return carry

    spread_shape = (2 * GROUP, GROUP * width)
    spread = jnp.where(
        lax.rem(lax.broadcasted_iota(jnp.int32, spread_shape, 0), GROUP)
        == lax.div(lax.broadcasted_iota(jnp.int32, spread_shape, 1), width),
        1.0,
        0.0,
    ).astype(BF16)

    def next_col_peaks(g, carry):
        columns = dot(lhs_pieces[g], spread, (0, 0))
        for k in range(GROUP):
            t = g * GROUP + k
            by_row = jnp.abs(tiles[t]) * columns[:, k * width : (k + 1) * width]
            col_local[pl.ds(t, 1), :] = jnp.max(by_row, axis=0, keepdims=True)
        return carry

    def next_row_peaks(g, carry):
        joined = row_local[...]
        for k in range(GROUP):
            t = g * GROUP + k
            by_col = jnp.abs(tiles[t]) * col_pieces[pl.ds(t, 1), :]
            joined = jnp.where(tile_lane == t, jnp.max(by_col, axis=1, keepdims=True), joined)
        row_local[...] = joined
        return carry

    def keep_halves(g, carry):
        for k in range(GROUP):
            t = g * GROUP + k
            halves[t, 0:width, :], halves[t, width : 2 * width, :] = split2(tiles[t])
        return carry

    def keep_turned(g, carry):
        for k in range(GROUP):
            t = g * GROUP + k
            turned[t, 0:width, :], turned[t, width : 2 * width, :] = split2(tiles[t].T)
        return carry

    def put_pieces(onehot, v):
        high, low = split2(v)
        shape = (slots // GROUP, GROUP, width)
        lhs_pieces[...] = jnp.concatenate(
            [dot(onehot, high).reshape(shape), dot(onehot, low).reshape(shape)], axis=1
        ).astype(BF16)

    def pad_rows(v):
        return jnp.concatenate([v, jnp.zeros((slots - v.shape[0], width), F32)], axis=0)

    row_scale = jnp.ones((slots, width), F32)
    col_scale = jnp.ones((cb, width), F32)
    for sweep in range(RUIZ):
        if sweep == 0:
            lax.fori_loop(0, groups, first_peaks, 0)
            pl.semaphore_wait(barrier, n_row + n_col - 2)
        else:
            col_pieces[...] = pick(col_pick, pad_rows(col_scale))

            @pl.when(jnp.logical_not(is_period))
            def _():
                put_pieces(row_pick, row_scale)
                lax.fori_loop(0, groups, next_col_peaks, 0)

            lax.fori_loop(0, groups, next_row_peaks, 0)
        row_peak = segment_max(pick(row_order, row_local[...], (1, 1)), row_masks, row_head)
        col_peak = segment_max(pick(col_order, col_local[...]), col_masks, col_head)
        col_box[sweep, my_row, 0:cb, :] = col_peak[0:cb]
        link_box[sweep, my_col] = row_peak[cb : cb + link]
        col_exchange(sweep).start()
        link_exchange(sweep).start()
        if sweep == 0:
            @pl.when(is_period)
            def _():
                put_pieces(row_pick, row_scale / jnp.sqrt(row_scale * row_peak + EPSILON))
                lax.fori_loop(0, groups, next_col_peaks, 0)

            lax.fori_loop(0, groups, keep_halves, 0)
        else:
            lax.fori_loop(0, groups, keep_turned, 0)
        col_exchange(sweep).finish()
        link_exchange(sweep).finish()
        link_peak = functools.reduce(jnp.maximum, [link_box[sweep, c] for c in range(n_col)])
        col_peak = functools.reduce(jnp.maximum, [col_box[sweep, r, 0:cb, :] for r in range(n_row)])
        row_peak = jnp.concatenate([row_peak[0:cb], link_peak, row_peak[cb + link :]], axis=0)
        row_scale = row_scale / jnp.sqrt(row_scale * row_peak + EPSILON)
        col_scale = col_scale / jnp.sqrt(col_scale * col_peak + EPSILON)

    def local_rows(ref):
        return pad_rows(jnp.concatenate([ref[pl.ds(period_base, cb), :], ref[link_base:rb, :]], axis=0))

    for copy in staged[1:]:
        copy.wait()
    cost = col_scale * objective_ref[...]
    bound = row_scale * local_rows(rhs_ref)
    low_scaled = lower_ref[...] / col_scale
    high_scaled = upper_ref[...] / col_scale
    primal = primal_ref[...] / col_scale
    dual = local_rows(dual_ref) / row_scale

    def fold(v):
        return jnp.sum(v.reshape(v.shape[0] // 8, 8, width), axis=0)

    norm_box[my_col, 0:8, :] = fold(cost * cost)
    norm_box[my_col, 8:16, :] = jnp.where(is_period, fold(bound[0:cb] * bound[0:cb]), 0.0)
    norm_exchange.start()

    pair_row = lax.rem(lax.broadcasted_iota(jnp.int32, (2 * GROUP, width), 0), GROUP)

    def product_step(weights, g, carry):
        lhs = lhs_pieces[g]
        both = jnp.concatenate([lhs, lhs], axis=1)
        joined = jnp.zeros((2 * GROUP, width), F32)
        for k in range(GROUP):
            joined = jnp.where(pair_row == k, dot(both, weights[g * GROUP + k]), joined)
        part = pl.ds(pl.multiple_of(g * GROUP, GROUP), GROUP)
        products[part, :] = joined[0:GROUP] + joined[GROUP:]
        return carry

    for iteration in range(ITERS):
        phase = RUIZ + iteration
        put_pieces(row_pick, row_scale * dual)
        lax.fori_loop(0, groups, functools.partial(product_step, halves), 0)
        col_box[phase, my_row, 0:cb, :] = pick(col_sum, products[...])[0:cb]
        if iteration == 0:
            norm_exchange.finish()
            cost_sum = functools.reduce(jnp.add, [norm_box[c, 0:8, :] for c in range(n_col)])
            bound_sum = functools.reduce(jnp.add, [norm_box[c, 8:16, :] for c in range(n_col)])
            link_bound = bound[cb : cb + link]
            col_box[phase, my_row, cb : cb + 8, :] = bound_sum + fold(link_bound * link_bound)
        col_exchange(phase).start()
        col_exchange(phase).finish()
        image = functools.reduce(jnp.add, [col_box[phase, r, 0:cb, :] for r in range(n_row)])
        if iteration == 0:
            bound_sum = functools.reduce(
                jnp.add, [col_box[phase, r, cb : cb + 8, :] for r in range(n_row)]
            )
            cost_total = jnp.sum(cost_sum, keepdims=True)
            bound_total = jnp.sum(bound_sum, keepdims=True)
            weight = jnp.sqrt(cost_total + EPSILON) / jnp.sqrt(bound_total + EPSILON)
            primal_step = step_ref[0] / weight
            dual_step = step_ref[0] * weight
        moved = jnp.clip(primal - primal_step * (cost - col_scale * image), low_scaled, high_scaled)
        put_pieces(col_pick, pad_rows(col_scale * (2.0 * moved - primal)))
        lax.fori_loop(0, groups, functools.partial(product_step, turned), 0)
        total = pick(row_sum, products[...])
        link_box[phase, my_col] = total[cb : cb + link]
        link_exchange(phase).start()
        primal = moved
        own = jnp.maximum(
            dual[0:cb] + dual_step * (bound[0:cb] - row_scale[0:cb] * total[0:cb]), 0.0
        )
        if iteration == ITERS - 1:

            @pl.when(is_period)
            def _():
                dual_box[my_period] = row_scale[0:cb] * own
                for d in range(1, n_col):
                    pltpu.make_async_remote_copy(
                        src_ref=dual_box.at[my_period],
                        dst_ref=dual_box.at[my_period],
                        send_sem=dual_send.at[d],
                        recv_sem=dual_recv.at[my_period],
                        device_id={"col": lax.rem(my_col + d, n_col)},
                        device_id_type=MESH,
                    ).start()

            primal_out[...] = col_scale * primal
        link_exchange(phase).finish()
        link_total = functools.reduce(jnp.add, [link_box[phase, c] for c in range(n_col)])
        span = slice(cb, cb + link)
        link_dual = jnp.maximum(
            dual[span] + dual_step * (bound[span] - row_scale[span] * link_total), 0.0
        )
        dual = pad_rows(jnp.concatenate([own, link_dual], axis=0))
    dual_out[link_base:rb, :] = (row_scale * dual)[cb : cb + link]
    for p in range(periods):
        owner = p * n_row + my_row

        @pl.when(owner != my_col)
        def _():
            pltpu.make_async_remote_copy(
                src_ref=dual_box.at[p],
                dst_ref=dual_box.at[p],
                send_sem=dual_send.at[0],
                recv_sem=dual_recv.at[p],
                device_id={"col": lax.rem(my_col + 1, n_col)},
                device_id_type=MESH,
            ).wait_recv()

        dual_out[p * cb : (p + 1) * cb, :] = dual_box[p]

    for phase in range(RUIZ + ITERS):
        col_exchange(phase).drain()
        link_exchange(phase).drain()
    norm_exchange.drain()

    @pl.when(is_period)
    def _():
        for d in range(1, n_col):
            pltpu.make_async_remote_copy(
                src_ref=dual_box.at[my_period],
                dst_ref=dual_box.at[my_period],
                send_sem=dual_send.at[d],
                recv_sem=dual_recv.at[my_period],
                device_id={"col": lax.rem(my_col + d, n_col)},
                device_id_type=MESH,
            ).wait_send()


def local(
    n_row,
    n_col,
    tile_values,
    tile_coords,
    tile_count,
    objective,
    lower,
    upper,
    rhs,
    primal_start,
    dual_start,
    step_size,
):
    width = tile_values.shape[-1]
    slots = tile_values.shape[2]
    cb = objective.shape[0] // width
    rb = rhs.shape[0] // width
    periods = n_col // n_row
    link = rb - periods * cb
    smem = pl.BlockSpec(memory_space=pltpu.SMEM)
    hbm = pl.BlockSpec(memory_space=pltpu.HBM)
    vmem = pl.BlockSpec(memory_space=pltpu.VMEM)
    phases = RUIZ + ITERS
    dma = pltpu.SemaphoreType.DMA
    primal, dual = pl.pallas_call(
        functools.partial(kernel, n_row, n_col, link),
        out_shape=(
            jax.ShapeDtypeStruct((cb, width), F32),
            jax.ShapeDtypeStruct((rb, width), F32),
        ),
        in_specs=[hbm, hbm, smem] + [hbm] * 6 + [smem],
        out_specs=(vmem, vmem),
        scratch_shapes=[
            pltpu.VMEM((slots, width, width), F32),
            pltpu.VMEM((slots, 2 * width, width), BF16),
            pltpu.VMEM((width, slots), F32),
            pltpu.VMEM((slots, width), F32),
            pltpu.VMEM((slots, width), F32),
            pltpu.VMEM((slots, 2 * width, width), BF16),
            pltpu.VMEM((slots // GROUP, 2 * GROUP, width), BF16),
            pltpu.VMEM((slots, width), F32),
            pltpu.VMEM((phases, n_row, cb + 8, width), F32),
            pltpu.VMEM((phases, n_col, link, width), F32),
            pltpu.VMEM((n_col, 16, width), F32),
            pltpu.VMEM((periods, cb, width), F32),
            pltpu.VMEM((2, slots), jnp.int32),
            pltpu.VMEM((cb, width), F32),
            pltpu.VMEM((cb, width), F32),
            pltpu.VMEM((cb, width), F32),
            pltpu.VMEM((rb, width), F32),
            pltpu.VMEM((cb, width), F32),
            pltpu.VMEM((rb, width), F32),
            dma((7,)),
            dma((slots // GROUP,)),
            dma((phases, n_row)),
            dma((phases, n_row)),
            dma((phases, n_col)),
            dma((phases, n_col)),
            dma((n_col,)),
            dma((n_col,)),
            dma((n_col,)),
            dma((periods,)),
        ],
        compiler_params=pltpu.CompilerParams(
            collective_id=0, has_side_effects=True, vmem_limit_bytes=60 * 1024 * 1024
        ),
        name="ruiz_pdhg",
    )(
        tile_values.reshape(slots, width, width),
        tile_coords.reshape(slots, 2).T,
        tile_count.reshape(1, 1),
        objective.reshape(cb, width),
        lower.reshape(cb, width),
        upper.reshape(cb, width),
        rhs.reshape(rb, width),
        primal_start.reshape(cb, width),
        dual_start.reshape(rb, width),
        step_size,
    )
    return primal.reshape(-1), dual.reshape(-1)


def solution(mesh):
    placed = (
        P("row", "col", None, None, None),
        P("row", "col", None, None),
        P("row", "col"),
        P("col"),
        P("col"),
        P("col"),
        P("row"),
        P("col"),
        P("row"),
        P(),
    )
    return jax.shard_map(
        functools.partial(local, mesh.shape["row"], mesh.shape["col"]),
        mesh=mesh,
        in_specs=placed,
        out_specs=(P("col"), P("row")),
        check_vma=False,
    )
```

```python
import functools

import jax
import jax.numpy as jnp
from jax import lax
from jax.experimental import pallas as pl
from jax.experimental.pallas import tpu as pltpu
from jax.sharding import PartitionSpec as P

RUIZ = 2
ITERS = 2
EPSILON = 1e-06
GROUP = 8
F32 = jnp.float32
BF16 = jnp.bfloat16
MESH = pl.DeviceIdType.MESH


def dot(a, b, dims=(1, 0)):
    return lax.dot_general(a, b, (((dims[0],), (dims[1],)), ((), ())), preferred_element_type=F32)


def split2(v):
    high = v.astype(BF16)
    return high, (v - high.astype(F32)).astype(BF16)


def pick(onehot, v, dims=(1, 0)):
    high = v.astype(BF16)
    rest = v - high.astype(F32)
    mid = rest.astype(BF16)
    low = (rest - mid.astype(F32)).astype(BF16)
    return (dot(onehot, high, dims) + dot(onehot, mid, dims)) + dot(onehot, low, dims)


def kernel(
    n_row,
    n_col,
    link,
    values_hbm,
    coords_hbm,
    count_ref,
    objective_hbm,
    lower_hbm,
    upper_hbm,
    rhs_hbm,
    primal_hbm,
    dual_hbm,
    step_ref,
    primal_out,
    dual_out,
    tiles,
    halves,
    row_local,
    col_local,
    col_pieces,
    turned,
    lhs_pieces,
    products,
    col_box,
    link_box,
    norm_box,
    dual_box,
    coords_ref,
    objective_ref,
    lower_ref,
    upper_ref,
    rhs_ref,
    primal_ref,
    dual_ref,
    input_sem,
    load_sem,
    col_send,
    col_recv,
    link_send,
    link_recv,
    norm_send,
    norm_recv,
    dual_send,
    dual_recv,
):
    slots, width = tiles.shape[0], tiles.shape[2]
    cb = objective_ref.shape[0]
    rb = rhs_ref.shape[0]
    periods = n_col // n_row
    link_base = rb - link
    my_row = lax.axis_index("row")
    my_col = lax.axis_index("col")
    is_period = lax.rem(my_col, n_row) == my_row
    my_period = my_col // n_row
    period_base = pl.multiple_of(my_period * cb, cb)
    groups = jnp.where(is_period, slots // GROUP, min(slots, cb) // GROUP)

    staged = [
        pltpu.make_async_copy(source, target, input_sem.at[i])
        for i, (source, target) in enumerate(
            (
                (coords_hbm, coords_ref),
                (objective_hbm, objective_ref),
                (lower_hbm, lower_ref),
                (upper_hbm, upper_ref),
                (rhs_hbm, rhs_ref),
                (primal_hbm, primal_ref),
                (dual_hbm, dual_ref),
            )
        )
    ]
    for copy in staged[:1]:
        copy.start()

    def load(g):
        part = pl.ds(pl.multiple_of(g * GROUP, GROUP), GROUP)
        return pltpu.make_async_copy(values_hbm.at[part], tiles.at[part], load_sem.at[g])

    def start_load(g, carry):
        load(g).start()
        return carry

    lax.fori_loop(0, groups, start_load, 0)
    for copy in staged[1:]:
        copy.start()

    barrier = pltpu.get_barrier_semaphore()
    for d in range(1, n_row):
        pl.semaphore_signal(
            barrier, inc=1, device_id={"row": lax.rem(my_row + d, n_row)}, device_id_type=MESH
        )
    for d in range(1, n_col):
        pl.semaphore_signal(
            barrier, inc=1, device_id={"col": lax.rem(my_col + d, n_col)}, device_id_type=MESH
        )

    def remote(box, send, recv, axis, target, index, source):
        return pltpu.make_async_remote_copy(
            src_ref=box.at[source],
            dst_ref=box.at[source],
            send_sem=send.at[index],
            recv_sem=recv.at[source],
            device_id={axis: target},
            device_id_type=MESH,
        )

    class Exchange:
        def __init__(self, box, send, recv, axis):
            self.n = n_row if axis == "row" else n_col
            self.me = my_row if axis == "row" else my_col
            self.args = (box, send, recv, axis)

        def start(self):
            for d in range(1, self.n):
                remote(*self.args, lax.rem(self.me + d, self.n), d, self.me).start()

        def finish(self):
            for d in range(1, self.n):
                other = lax.rem(self.me + self.n - d, self.n)
                remote(*self.args, other, d, other).wait_recv()

        def drain(self):
            for d in range(1, self.n):
                remote(*self.args, lax.rem(self.me + d, self.n), d, self.me).wait_send()

    def col_exchange(phase):
        return Exchange(col_box.at[phase], col_send.at[phase], col_recv.at[phase], "row")

    def link_exchange(phase):
        return Exchange(link_box.at[phase], link_send.at[phase], link_recv.at[phase], "col")

    norm_exchange = Exchange(norm_box, norm_send, norm_recv, "col")

    square = (slots, slots)
    lane = lax.broadcasted_iota(jnp.int32, square, 1)
    sublane = lax.broadcasted_iota(jnp.int32, square, 0)
    lane_f = lane.astype(F32)
    for copy in staged[:1]:
        copy.wait()
    used = sublane < count_ref[0, 0]
    coords = coords_ref[...].astype(F32)
    block_row = jnp.broadcast_to(coords[0:1, :], square).T.astype(jnp.int32)
    block_col = jnp.broadcast_to(coords[1:2, :], square).T.astype(jnp.int32)
    local_row = jnp.where(is_period, block_row - period_base, block_row - (link_base - cb))

    def layout(place):
        place = jnp.where(used, place, 2 * slots - 1)
        onehot = jnp.where(place == lane, 1.0, 0.0)
        place_f = place.astype(F32)
        key = place_f * slots + sublane.astype(F32)
        rank = jnp.sum(jnp.where(key.T < key, 1.0, 0.0), axis=1, keepdims=True)
        order = jnp.where(jnp.broadcast_to(rank, square) == lane_f, 1.0, 0.0).T
        placed = jnp.broadcast_to(jnp.sum(order * place_f.T, axis=1, keepdims=True), square)
        masks = []
        d = 1
        while d < slots:
            masks.append(jnp.where(pltpu.roll(placed, slots - d, axis=0) == placed, 1.0, 0.0))
            d *= 2
        first = (pltpu.roll(placed, 1, axis=0) != placed) | (sublane == 0)
        head = jnp.where((placed == lane_f) & first, 1.0, 0.0).T
        return onehot.astype(BF16), onehot.T.astype(BF16), order.astype(BF16), masks, head.astype(BF16)

    row_pick, row_sum, row_order, row_masks, row_head = layout(local_row)
    col_pick, col_sum, col_order, col_masks, col_head = layout(block_col)

    def segment_max(ordered, masks, head):
        d = 1
        for mask in masks:
            ordered = jnp.maximum(ordered, mask * pltpu.roll(ordered, slots - d, axis=0))
            d *= 2
        return pick(head, ordered)

    row_local[...] = jnp.zeros_like(row_local)
    col_local[...] = jnp.zeros_like(col_local)
    products[...] = jnp.zeros_like(products)
    tile_lane = lax.broadcasted_iota(jnp.int32, (width, slots), 1)

    def first_peaks(g, carry):
        load(g).wait()
        joined = row_local[...]
        for k in range(GROUP):
            t = g * GROUP + k
            tile = tiles[t]
            size = jnp.abs(tile)
            col_local[pl.ds(t, 1), :] = jnp.max(size, axis=0, keepdims=True)
            joined = jnp.where(tile_lane == t, jnp.max(size, axis=1, keepdims=True), joined)
        row_local[...] = joined
        return carry

    spread_shape = (2 * GROUP, GROUP * width)
    spread = jnp.where(
        lax.rem(lax.broadcasted_iota(jnp.int32, spread_shape, 0), GROUP)
        == lax.div(lax.broadcasted_iota(jnp.int32, spread_shape, 1), width),
        1.0,
        0.0,
    ).astype(BF16)

    def next_col_peaks(g, carry):
        columns = dot(lhs_pieces[g], spread, (0, 0))
        for k in range(GROUP):
            t = g * GROUP + k
            by_row = jnp.abs(tiles[t]) * columns[:, k * width : (k + 1) * width]
            col_local[pl.ds(t, 1), :] = jnp.max(by_row, axis=0, keepdims=True)
        return carry

    def next_row_peaks(g, carry):
        joined = row_local[...]
        for k in range(GROUP):
            t = g * GROUP + k
            by_col = jnp.abs(tiles[t]) * col_pieces[pl.ds(t, 1), :]
            joined = jnp.where(tile_lane == t, jnp.max(by_col, axis=1, keepdims=True), joined)
        row_local[...] = joined
        return carry

    def keep_halves(g, carry):
        for k in range(GROUP):
            t = g * GROUP + k
            halves[t, 0:width, :], halves[t, width : 2 * width, :] = split2(tiles[t])
        return carry

    def keep_turned(g, carry):
        for k in range(GROUP):
            t = g * GROUP + k
            turned[t, 0:width, :], turned[t, width : 2 * width, :] = split2(tiles[t].T)
        return carry

    def put_pieces(onehot, v):
        high, low = split2(v)
        shape = (slots // GROUP, GROUP, width)
        lhs_pieces[...] = jnp.concatenate(
            [dot(onehot, high).reshape(shape), dot(onehot, low).reshape(shape)], axis=1
        ).astype(BF16)

    pair_row = lax.rem(lax.broadcasted_iota(jnp.int32, (2 * GROUP, width), 0), GROUP)

    def product_step(weights, g, carry):
        lhs = lhs_pieces[g]
        both = jnp.concatenate([lhs, lhs], axis=1)
        joined = jnp.zeros((2 * GROUP, width), F32)
        for k in range(GROUP):
            joined = jnp.where(pair_row == k, dot(both, weights[g * GROUP + k]), joined)
        part = pl.ds(pl.multiple_of(g * GROUP, GROUP), GROUP)
        products[part, :] = joined[0:GROUP] + joined[GROUP:]
        return carry

    def pad_rows(v):
        return jnp.concatenate([v, jnp.zeros((slots - v.shape[0], width), F32)], axis=0)

    def local_rows(ref):
        return pad_rows(jnp.concatenate([ref[pl.ds(period_base, cb), :], ref[link_base:rb, :]], axis=0))

    def fold(v):
        return jnp.sum(v.reshape(v.shape[0] // 8, 8, width), axis=0)

    row_scale = jnp.ones((slots, width), F32)
    col_scale = jnp.ones((cb, width), F32)
    for sweep in range(RUIZ):
        if sweep == 0:
            lax.fori_loop(0, groups, first_peaks, 0)
            pl.semaphore_wait(barrier, n_row + n_col - 2)
            for copy in staged[1:]:
                copy.wait()
        else:
            col_pieces[...] = pick(col_pick, pad_rows(col_scale))

            @pl.when(jnp.logical_not(is_period))
            def _():
                put_pieces(row_pick, row_scale)
                lax.fori_loop(0, groups, next_col_peaks, 0)

            lax.fori_loop(0, groups, next_row_peaks, 0)
        row_peak = segment_max(pick(row_order, row_local[...], (1, 1)), row_masks, row_head)
        col_peak = segment_max(pick(col_order, col_local[...]), col_masks, col_head)
        col_box[sweep, my_row, 0:cb, :] = col_peak[0:cb]
        link_box[sweep, my_col] = row_peak[cb : cb + link]
        if sweep == RUIZ - 1:
            known = row_scale[0:cb] / jnp.sqrt(row_scale[0:cb] * row_peak[0:cb] + EPSILON)
            known = known * rhs_ref[pl.ds(period_base, cb), :]
            col_box[sweep, my_row, cb : cb + 8, :] = jnp.where(is_period, fold(known * known), 0.0)
        col_exchange(sweep).start()
        link_exchange(sweep).start()
        if sweep == 0:
            @pl.when(is_period)
            def _():
                put_pieces(row_pick, row_scale / jnp.sqrt(row_scale * row_peak + EPSILON))
                lax.fori_loop(0, groups, next_col_peaks, 0)

            lax.fori_loop(0, groups, keep_halves, 0)
        else:
            lax.fori_loop(0, groups, keep_turned, 0)
            put_pieces(row_pick, local_rows(dual_ref))
            lax.fori_loop(0, groups, functools.partial(product_step, halves), 0)
            col_box[RUIZ, my_row, 0:cb, :] = pick(col_sum, products[...])[0:cb]
        col_exchange(sweep).finish()
        link_exchange(sweep).finish()
        link_peak = functools.reduce(jnp.maximum, [link_box[sweep, c] for c in range(n_col)])
        col_peak = functools.reduce(jnp.maximum, [col_box[sweep, r, 0:cb, :] for r in range(n_row)])
        row_peak = jnp.concatenate([row_peak[0:cb], link_peak, row_peak[cb + link :]], axis=0)
        row_scale = row_scale / jnp.sqrt(row_scale * row_peak + EPSILON)
        col_scale = col_scale / jnp.sqrt(col_scale * col_peak + EPSILON)

    cost = col_scale * objective_ref[...]
    bound = row_scale * local_rows(rhs_ref)
    low_scaled = lower_ref[...] / col_scale
    high_scaled = upper_ref[...] / col_scale
    primal = primal_ref[...] / col_scale
    dual = local_rows(dual_ref) / row_scale

    norm_box[my_col, 0:8, :] = fold(cost * cost)
    norm_box[my_col, 8:16, :] = functools.reduce(
        jnp.add, [col_box[RUIZ - 1, r, cb : cb + 8, :] for r in range(n_row)]
    )
    norm_exchange.start()

    for iteration in range(ITERS):
        phase = RUIZ + iteration
        if iteration == 0:
            link_bound = bound[cb : cb + link]
            col_box[phase, my_row, cb : cb + 8, :] = fold(link_bound * link_bound)
        else:
            put_pieces(row_pick, row_scale * dual)
            lax.fori_loop(0, groups, functools.partial(product_step, halves), 0)
            col_box[phase, my_row, 0:cb, :] = pick(col_sum, products[...])[0:cb]
        col_exchange(phase).start()
        col_exchange(phase).finish()
        image = functools.reduce(jnp.add, [col_box[phase, r, 0:cb, :] for r in range(n_row)])
        if iteration == 0:
            norm_exchange.finish()
            cost_sum = functools.reduce(jnp.add, [norm_box[c, 0:8, :] for c in range(n_col)])
            bound_sum = functools.reduce(
                jnp.add,
                [norm_box[c, 8:16, :] for c in range(n_col)]
                + [col_box[phase, r, cb : cb + 8, :] for r in range(n_row)],
            )
            cost_total = jnp.sum(cost_sum, keepdims=True)
            bound_total = jnp.sum(bound_sum, keepdims=True)
            weight = jnp.sqrt(cost_total + EPSILON) / jnp.sqrt(bound_total + EPSILON)
            primal_step = step_ref[0] / weight
            dual_step = step_ref[0] * weight
        moved = jnp.clip(primal - primal_step * (cost - col_scale * image), low_scaled, high_scaled)
        put_pieces(col_pick, pad_rows(col_scale * (2.0 * moved - primal)))
        lax.fori_loop(0, groups, functools.partial(product_step, turned), 0)
        total = pick(row_sum, products[...])
        link_box[phase, my_col] = total[cb : cb + link]
        link_exchange(phase).start()
        primal = moved
        own = jnp.maximum(
            dual[0:cb] + dual_step * (bound[0:cb] - row_scale[0:cb] * total[0:cb]), 0.0
        )
        if iteration == ITERS - 1:

            @pl.when(is_period)
            def _():
                dual_box[my_period] = row_scale[0:cb] * own
                for d in range(1, n_col):
                    pltpu.make_async_remote_copy(
                        src_ref=dual_box.at[my_period],
                        dst_ref=dual_box.at[my_period],
                        send_sem=dual_send.at[d],
                        recv_sem=dual_recv.at[my_period],
                        device_id={"col": lax.rem(my_col + d, n_col)},
                        device_id_type=MESH,
                    ).start()

            primal_out[...] = col_scale * primal
        link_exchange(phase).finish()
        link_total = functools.reduce(jnp.add, [link_box[phase, c] for c in range(n_col)])
        span = slice(cb, cb + link)
        link_dual = jnp.maximum(
            dual[span] + dual_step * (bound[span] - row_scale[span] * link_total), 0.0
        )
        dual = pad_rows(jnp.concatenate([own, link_dual], axis=0))
    dual_out[link_base:rb, :] = (row_scale * dual)[cb : cb + link]
    for p in range(periods):
        owner = p * n_row + my_row

        @pl.when(owner != my_col)
        def _():
            pltpu.make_async_remote_copy(
                src_ref=dual_box.at[p],
                dst_ref=dual_box.at[p],
                send_sem=dual_send.at[0],
                recv_sem=dual_recv.at[p],
                device_id={"col": lax.rem(my_col + 1, n_col)},
                device_id_type=MESH,
            ).wait_recv()

        dual_out[p * cb : (p + 1) * cb, :] = dual_box[p]

    for phase in range(RUIZ + ITERS):
        col_exchange(phase).drain()
        link_exchange(phase).drain()
    norm_exchange.drain()

    @pl.when(is_period)
    def _():
        for d in range(1, n_col):
            pltpu.make_async_remote_copy(
                src_ref=dual_box.at[my_period],
                dst_ref=dual_box.at[my_period],
                send_sem=dual_send.at[d],
                recv_sem=dual_recv.at[my_period],
                device_id={"col": lax.rem(my_col + d, n_col)},
                device_id_type=MESH,
            ).wait_send()


def local(
    n_row,
    n_col,
    tile_values,
    tile_coords,
    tile_count,
    objective,
    lower,
    upper,
    rhs,
    primal_start,
    dual_start,
    step_size,
):
    width = tile_values.shape[-1]
    slots = tile_values.shape[2]
    cb = objective.shape[0] // width
    rb = rhs.shape[0] // width
    periods = n_col // n_row
    link = rb - periods * cb
    smem = pl.BlockSpec(memory_space=pltpu.SMEM)
    hbm = pl.BlockSpec(memory_space=pltpu.HBM)
    vmem = pl.BlockSpec(memory_space=pltpu.VMEM)
    phases = RUIZ + ITERS
    dma = pltpu.SemaphoreType.DMA
    primal, dual = pl.pallas_call(
        functools.partial(kernel, n_row, n_col, link),
        out_shape=(
            jax.ShapeDtypeStruct((cb, width), F32),
            jax.ShapeDtypeStruct((rb, width), F32),
        ),
        in_specs=[hbm, hbm, smem] + [hbm] * 6 + [smem],
        out_specs=(vmem, vmem),
        scratch_shapes=[
            pltpu.VMEM((slots, width, width), F32),
            pltpu.VMEM((slots, 2 * width, width), BF16),
            pltpu.VMEM((width, slots), F32),
            pltpu.VMEM((slots, width), F32),
            pltpu.VMEM((slots, width), F32),
            pltpu.VMEM((slots, 2 * width, width), BF16),
            pltpu.VMEM((slots // GROUP, 2 * GROUP, width), BF16),
            pltpu.VMEM((slots, width), F32),
            pltpu.VMEM((phases, n_row, cb + 8, width), F32),
            pltpu.VMEM((phases, n_col, link, width), F32),
            pltpu.VMEM((n_col, 16, width), F32),
            pltpu.VMEM((periods, cb, width), F32),
            pltpu.VMEM((2, slots), jnp.int32),
            pltpu.VMEM((cb, width), F32),
            pltpu.VMEM((cb, width), F32),
            pltpu.VMEM((cb, width), F32),
            pltpu.VMEM((rb, width), F32),
            pltpu.VMEM((cb, width), F32),
            pltpu.VMEM((rb, width), F32),
            dma((7,)),
            dma((slots // GROUP,)),
            dma((phases, n_row)),
            dma((phases, n_row)),
            dma((phases, n_col)),
            dma((phases, n_col)),
            dma((n_col,)),
            dma((n_col,)),
            dma((n_col,)),
            dma((periods,)),
        ],
        compiler_params=pltpu.CompilerParams(
            collective_id=0, has_side_effects=True, vmem_limit_bytes=60 * 1024 * 1024
        ),
        name="ruiz_pdhg",
    )(
        tile_values.reshape(slots, width, width),
        tile_coords.reshape(slots, 2).T,
        tile_count.reshape(1, 1),
        objective.reshape(cb, width),
        lower.reshape(cb, width),
        upper.reshape(cb, width),
        rhs.reshape(rb, width),
        primal_start.reshape(cb, width),
        dual_start.reshape(rb, width),
        step_size,
    )
    return primal.reshape(-1), dual.reshape(-1)


def solution(mesh):
    placed = (
        P("row", "col", None, None, None),
        P("row", "col", None, None),
        P("row", "col"),
        P("col"),
        P("col"),
        P("col"),
        P("row"),
        P("col"),
        P("row"),
        P(),
    )
    return jax.shard_map(
        functools.partial(local, mesh.shape["row"], mesh.shape["col"]),
        mesh=mesh,
        in_specs=placed,
        out_specs=(P("col"), P("row")),
        check_vma=False,
    )
```
